32 devices in a mesh: dp: 4 (over z), tm: 4 (over y, x), rows: 2 (over core).
Axes of the slice: x: 2, y: 2, z: 4, core: 2. Of those that a mesh axis runs over, the one named last changes fastest.
Arguments:
- queries: bfloat16 [4, 4, 1, 1, 384, 1536], P('dp', 'tm', None, None, None, 'rows'), may hold values from -44 to 44
- keys_values: bfloat16 [4, 4, 1, 1, 384, 2, 1536], P('dp', 'tm', None, None, None, None, 'rows'), may hold values from -5 to 5
- window_offsets: int32 [4, 4, 1, 1, 3], P('dp', 'tm'), may hold values from 0 to 26, as said below
- out_weight: bfloat16 [1536, 1536], P(('rows', 'dp')), may hold values from -0.15625 to 0.15625
- gate: float32 [4, 1536], P('dp'), may hold values from 3 to 30
Outputs:
- mixed: bfloat16 [4, 4, 1, 1, 384, 1536], P('dp', 'tm', None, None, 'rows')
The draws below stay inside these ranges and needn't reach their ends.
Inputs may be any that keep to these rules, and one draw needn't show every extreme that they name: `window_offsets`: entry 0 of every row is 13; the other 2 entries are distinct offsets other than 13, which may point outside the grid.
All inputs are finite; a program needn't handle non-finite values.
Results may differ from the reference program's by a relative error of at most 0.015.
Values may be sent and summed in bfloat16 or wider, within the bound.
A program may use at most 64 MiB of HBM per device.

```python
import math
import jax
import jax.numpy as jnp
from jax import lax

HEADS = 12
HD = 128
C = 1536
DOUT = 1536
TL = 384
KEEP = 3
NHT = 1
WT = 1
NTT = 4
VIDEOS = 4


def draw_both(key):
    width = HEADS * HD
    shape_q = (VIDEOS, NTT, NHT, WT, TL, width)
    shape_kv = (VIDEOS, NTT, NHT, WT, TL, 2, width)
    key_q = jax.random.fold_in(key, 11)
    key_kv = jax.random.fold_in(key, 12)
    query = jnp.clip(jax.random.normal(key_q, shape_q, jnp.float32), -5.0, 5.0)
    pairs = jnp.clip(jax.random.normal(key_kv, shape_kv, jnp.float32), -5.0, 5.0)
    return (query.astype(jnp.bfloat16), pairs.astype(jnp.bfloat16))


def draw_queries(key, part):
    return draw_both(key)[0]


def draw_keys_values(key, part):
    return draw_both(key)[1]


def draw_window_offsets(key, part):
    rows_shape = (VIDEOS, NTT, NHT, WT, 26)
    scores = jax.random.randint(jax.random.fold_in(key, 21), rows_shape, 0, 1 << 20)
    scores = scores * 32 + jnp.arange(26, dtype=jnp.int32)
    order = jnp.argsort(scores, axis=-1, stable=True).astype(jnp.int32)
    others = order[..., :KEEP - 1]
    others = others + (others >= 13).astype(jnp.int32)
    centre = jnp.full((VIDEOS, NTT, NHT, WT, 1), 13, jnp.int32)
    return jnp.concatenate([centre, others], axis=-1)


def shard_levels(key, extent, cuts, least, top_value):
    factor_of = 1.0
    for position, blocks in cuts:
        heights = jax.random.uniform(jax.random.fold_in(jax.random.fold_in(key, 6), position), (blocks,), jnp.float32, least / len(cuts), top_value / len(cuts))
        factor_of = factor_of * jnp.repeat(jnp.exp(heights), extent[position] // blocks).reshape((-1,) + (1,) * (len(extent) - 1 - position))
    return factor_of


def centred(rng, dims, scale, most, cuts=(), held_as=jnp.bfloat16):
    drawn = jax.random.normal(rng, dims, jnp.float32) * scale
    if len(cuts) > 0:
        drawn = shard_levels(rng, dims, cuts, -0.22, 0.18) * drawn
    return jnp.clip(drawn, min=-most, max=most).astype(held_as)


def setup_inputs(seed: int = 0) -> dict:
    key_list = jax.random.split(jax.random.key(seed), 6)
    return {
        "queries": draw_queries(jax.random.fold_in(key_list[5], 71), 0),
        "keys_values": draw_keys_values(jax.random.fold_in(key_list[5], 71), 0),
        "window_offsets": draw_window_offsets(jax.random.fold_in(key_list[5], 71), 0),
        "out_weight": centred(key_list[3], (C, DOUT), C ** -0.5, 0.15625, ((0, 8),)),
        "gate": jnp.clip(jnp.exp(math.log(30.0) - 2.3025851 * jax.random.uniform(key_list[4], (VIDEOS, DOUT), jnp.float32) ** shard_levels(key_list[4], (VIDEOS, DOUT), ((0, 4),), -0.2, 0.2)), 3.0, 30.0),
    }


def tile_attend(query_tile, key_tiles, live_row):
    scale = float(HD) ** -0.5
    query = query_tile.astype(jnp.float32).reshape(TL, HEADS, HD)
    keys = key_tiles[:, :, 0, :].astype(jnp.float32).reshape(KEEP * TL, HEADS, HD)
    values = key_tiles[:, :, 1, :].astype(jnp.float32).reshape(KEEP * TL, HEADS, HD)
    scores = jnp.einsum("qnd,knd->nqk", query, keys) * scale
    mask = jnp.repeat(live_row, TL)[None, None, :]
    top = jnp.max(jnp.where(mask, scores, -jnp.inf), axis=2, keepdims=True)
    prob = jnp.where(mask, jnp.exp(scores - top), 0.0)
    total = jnp.sum(prob, axis=2, keepdims=True)
    weights = (prob / total).astype(jnp.bfloat16).astype(jnp.float32)
    acc = jnp.einsum("nqk,knd->qnd", weights, values)
    return acc.astype(jnp.bfloat16).reshape(TL, HEADS * HD)


def one_video(args):
    query_in, kv_in, offsets, gate_row, out_weight = args
    width = HEADS * HD
    tiles = NTT * NHT * WT
    kv_flat = kv_in.reshape(tiles, TL, 2, width)
    q_flat = query_in.reshape(tiles, TL, width)
    time_pos = jnp.arange(NTT, dtype=jnp.int32)[:, None, None, None]
    row_pos = jnp.arange(NHT, dtype=jnp.int32)[None, :, None, None]
    col_pos = jnp.arange(WT, dtype=jnp.int32)[None, None, :, None]
    first = offsets // 9 - 1
    second = (offsets // 3) % 3 - 1
    third = offsets % 3 - 1
    near_t = time_pos + first
    near_h = row_pos + second
    near_w = col_pos + third
    inside = (near_t >= 0) & (near_t < NTT) & (near_h >= 0) & (near_h < NHT) & (near_w >= 0) & (near_w < WT)
    index = (jnp.clip(near_t, 0, NTT - 1) * (NHT * WT) + jnp.clip(near_h, 0, NHT - 1) * WT + jnp.clip(near_w, 0, WT - 1)).astype(jnp.int32)
    index = index.reshape(tiles, KEEP)
    inside = inside.reshape(tiles, KEEP)

    def per_tile(items):
        query_tile, index_row, live_row = items
        key_tiles = jnp.take(kv_flat, index_row, axis=0)
        return tile_attend(query_tile, key_tiles, live_row)

    attended = lax.map(per_tile, (q_flat, index, inside)).reshape(tiles * TL, width)
    projection = jnp.dot(attended, out_weight, preferred_element_type=jnp.float32)
    mixed = (gate_row[None, :] * projection).astype(jnp.bfloat16)
    return mixed.reshape(NTT, NHT, WT, TL, DOUT)


def reference(queries, keys_values, window_offsets, out_weight, gate):
    def per_video(args):
        query_in, kv_in, offsets, gate_row = args
        return one_video((query_in, kv_in, offsets, gate_row, out_weight))
    return lax.map(per_video, (queries, keys_values, window_offsets, gate))
```

```python
import functools
import math

import jax
import jax.numpy as jnp
from jax import lax
from jax.experimental import pallas as pl
from jax.experimental.pallas import tpu as pltpu
from jax.sharding import PartitionSpec as P

HD = 128
MESH = pl.DeviceIdType.MESH
PARTS = 2
PLAN = {1: 1, 2: 1, 4: 1, 5: 1}


def kernel(
    ndp,
    ntm,
    heads,
    off_ref,
    q_ref,
    kv_ref,
    w_ref,
    gate_ref,
    out_ref,
    a_buf,
    b_buf,
    wbuf,
    att,
    att_send,
    a_send,
    a_recv,
    b_send,
    b_recv,
    z_send,
    z_recv,
    c_send,
    c_recv,
    own_send,
    own_recv,
    own_local,
    att_sem,
):
    i = lax.axis_index("dp")
    t = lax.axis_index("tm")
    r = lax.axis_index("rows")
    other = 1 - r
    relay = ntm == 4
    odd = t % 2
    partner = t + 1 - 2 * odd
    beyond = t - 1 + 2 * odd
    has_b = jnp.logical_and(beyond >= 0, beyond < ntm)
    if relay:
        b_target = (t + 2) % 4
        b_sends = jnp.logical_not(has_b)
        greets_b = t >= 0
    else:
        b_target = jnp.clip(beyond, 0, ntm - 1)
        b_sends = has_b
        greets_b = has_b
    has_left = i > 0
    has_right = i < ndp - 1
    left = jnp.maximum(i - 1, 0)
    right = jnp.minimum(i + 1, ndp - 1)
    band = out_ref.shape[0]
    rows = w_ref.shape[0]
    piece = rows // PARTS
    events = PARTS * (ndp - 1)

    barrier = pltpu.get_barrier_semaphore()

    def greet(device):
        pl.semaphore_signal(barrier, inc=1, device_id=device, device_id_type=MESH)

    greet({"rows": other})
    greet({"tm": partner})

    @pl.when(greets_b)
    def _():
        greet({"tm": b_target})

    @pl.when(has_left)
    def _():
        greet({"dp": left})

    @pl.when(has_right)
    def _():
        greet({"dp": right})

    peers = 2
    for present in (greets_b, has_left, has_right):
        peers = peers + jnp.where(present, 1, 0)
    pl.semaphore_wait(barrier, peers)

    def remote(src, dst, send, recv, device):
        return pltpu.make_async_remote_copy(
            src_ref=src, dst_ref=dst, send_sem=send, recv_sem=recv, device_id=device, device_id_type=MESH
        )

    def a_copy(h):
        return remote(kv_ref.at[h], a_buf.at[h], a_send.at[h], a_recv.at[h], {"tm": partner})

    def b_copy(h):
        src = a_buf if relay else kv_ref
        return remote(src.at[h], b_buf.at[h], b_send.at[h], b_recv.at[h], {"tm": b_target})

    def place(half, shard, part):
        start = pl.multiple_of((half * ndp + shard) * rows + part * piece, 16)
        return wbuf.at[pl.ds(start, piece)]

    def own_piece(part):
        return w_ref.at[pl.ds(part * piece, piece)]

    def z_copy(src, shard, part, side, event):
        target = right if side == 0 else left
        return remote(
            src, place(r, shard, part), z_send.at[side, event], z_recv.at[side, event], {"dp": target}
        )

    def c_copy(shard, part, side, event):
        spot = place(r, shard, part)
        return remote(spot, spot, c_send.at[side, event], c_recv.at[side, event], {"rows": other})

    def shard_of(step, side):
        return i - 1 - step if side == 0 else i + 1 + step

    def valid(step, side):
        shard = shard_of(step, side)
        return shard >= 0 if side == 0 else shard < ndp

    sends_on = (has_right, has_left)

    for h in range(min(2, heads)):
        a_copy(h).start()
    for part in range(PARTS):
        for side in (0, 1):
            @pl.when(sends_on[side])
            def _():
                z_copy(own_piece(part), i, part, side, part).start()
    own_spot = wbuf.at[pl.ds(pl.multiple_of((r * ndp + i) * rows, 16), rows)]
    own_copy = pltpu.make_async_copy(w_ref, own_spot, own_local)
    own_copy.start()
    own_across = remote(w_ref, own_spot, own_send, own_recv, {"rows": other})
    own_across.start()
    if not relay:
        @pl.when(b_sends)
        def _():
            for h in range(heads):
                b_copy(h).start()

    @pl.when(jnp.logical_not(has_b))
    def _():
        b_buf[...] = jnp.zeros_like(b_buf)

    def weight_event(event):
        step, part = event // PARTS, event % PARTS
        for side in (0, 1):
            @pl.when(valid(step, side))
            def _():
                shard = shard_of(step, side)
                spot = place(r, shard, part)
                z_copy(spot, shard, part, side, event).wait_recv()

                @pl.when(sends_on[side])
                def _():
                    z_copy(spot, shard, part, side, event + PARTS).start()

                c_copy(shard, part, side, event).start()

    def is_live(code):
        hit = off_ref[0] == code
        for k in range(1, off_ref.shape[0]):
            hit = jnp.logical_or(hit, off_ref[k] == code)
        return hit

    low = is_live(4)
    high = is_live(22)
    a_live = jnp.logical_or(jnp.logical_and(low, odd == 1), jnp.logical_and(high, odd == 0))
    b_live = jnp.logical_or(jnp.logical_and(low, odd == 0), jnp.logical_and(high, odd == 1))
    b_live = jnp.logical_and(b_live, has_b)
    dead = jnp.float32(-jnp.inf)
    a_bias = jnp.where(a_live, jnp.float32(0), dead)
    b_bias = jnp.where(b_live, jnp.float32(0), dead)
    factor = HD**-0.5 * math.log2(math.e)

    def score(q, keys):
        return lax.dot_general(
            q, keys, (((1,), (1,)), ((), ())), preferred_element_type=jnp.float32
        )

    def attend(h, which):
        q = q_ref[pl.ds(pl.multiple_of(which * band, 16), band), h * HD : (h + 1) * HD]
        parts = (
            score(q, kv_ref[h, 0]),
            score(q, a_buf[h, 0]) + a_bias,
            score(q, b_buf[h, 0]) + b_bias,
        )
        top = functools.reduce(
            jnp.maximum, [jnp.max(s, axis=1, keepdims=True) for s in parts]
        )
        total = 0.0
        acc = 0.0
        for s, held in zip(parts, (kv_ref, a_buf, b_buf)):
            p = jnp.exp2((s - top) * factor)
            total = total + jnp.sum(p, axis=1, keepdims=True)
            acc = acc + jnp.dot(
                p.astype(jnp.bfloat16), held[h, 1], preferred_element_type=jnp.float32
            )
        return (acc / total).astype(jnp.bfloat16)

    done = 0
    for h in range(heads + 1):
        if h < heads:
            a_copy(h).wait_recv()
            if h + 2 < heads:
                a_copy(h + 2).start()
            if relay:
                @pl.when(b_sends)
                def _():
                    b_copy(h).start()
        if ndp == 4:
            for _ in range(PLAN.get(h, 0)):
                weight_event(done)
                done += 1
        if h > 0:
            g = h - 1

            @pl.when(has_b)
            def _():
                b_copy(g).wait_recv()

            columns = pl.ds(g * HD, HD)
            att_send[:, columns] = attend(g, other)
            att[r, :, columns] = attend(g, r)

    across = remote(att_send, att.at[r], att_sem.at[0], att_sem.at[1], {"rows": other})
    across.start()

    def later(event, carry):
        weight_event(event)
        return carry

    lax.fori_loop(done, events, later, 0)

    own_copy.wait()
    own_across.wait_recv()
    across.wait_recv()

    def settle(event, carry):
        step, part = event // PARTS, event % PARTS
        for side in (0, 1):
            @pl.when(valid(step, side))
            def _():
                c_copy(shard_of(step, side), part, side, event).wait_recv()
        return carry

    lax.fori_loop(0, events, settle, 0)

    half = wbuf.shape[0] // 2
    width = out_ref.shape[1]
    tile = 512 if width % 512 == 0 else width
    for start in range(0, width, tile):
        columns = pl.ds(start, tile)
        product = jnp.dot(att[0], wbuf[:half, columns], preferred_element_type=jnp.float32)
        product += jnp.dot(att[1], wbuf[half:, columns], preferred_element_type=jnp.float32)
        out_ref[:, columns] = (gate_ref[:, columns] * product).astype(out_ref.dtype)

    for h in range(heads):
        a_copy(h).wait_send()

    @pl.when(b_sends)
    def _():
        for h in range(heads):
            b_copy(h).wait_send()

    own_across.wait_send()
    across.wait_send()

    def sent_own(part, carry):
        for side in (0, 1):
            @pl.when(sends_on[side])
            def _():
                z_copy(own_piece(part), i, part, side, part).wait_send()
        return carry

    for part in range(PARTS):
        sent_own(part, 0)

    def sent(event, carry):
        step, part = event // PARTS, event % PARTS
        for side in (0, 1):
            @pl.when(valid(step, side))
            def _():
                shard = shard_of(step, side)
                c_copy(shard, part, side, event).wait_send()

                @pl.when(sends_on[side])
                def _():
                    z_copy(place(r, shard, part), shard, part, side, event + PARTS).wait_send()
        return carry

    lax.fori_loop(0, events, sent, 0)


def local(queries, keys_values, window_offsets, out_weight, gate):
    tl, width = queries.shape[4], queries.shape[5]
    heads = width // HD
    ndp, ntm, bands = lax.axis_size("dp"), lax.axis_size("tm"), lax.axis_size("rows")
    assert queries.shape[2] == queries.shape[3] == 1 and bands == 2 and ntm % 2 == 0
    band = tl // bands
    rows, dout = out_weight.shape
    events = PARTS * (ndp - 1)
    kv = keys_values.reshape(tl, 2, heads, HD).transpose(2, 1, 0, 3)
    bf16 = jnp.bfloat16
    vmem = pl.BlockSpec(memory_space=pltpu.VMEM)
    dma = pltpu.SemaphoreType.DMA
    mixed = pl.pallas_call(
        functools.partial(kernel, ndp, ntm, heads),
        out_shape=jax.ShapeDtypeStruct((band, dout), bf16),
        in_specs=[pl.BlockSpec(memory_space=pltpu.SMEM), vmem, vmem, vmem, vmem],
        out_specs=vmem,
        scratch_shapes=[
            pltpu.VMEM((heads, 2, tl, HD), bf16),
            pltpu.VMEM((heads, 2, tl, HD), bf16),
            pltpu.VMEM((2 * ndp * rows, dout), bf16),
            pltpu.VMEM((2, band, width), bf16),
            pltpu.VMEM((band, width), bf16),
            dma((heads,)),
            dma((heads,)),
            dma((heads,)),
            dma((heads,)),
            dma((2, events + PARTS)),
            dma((2, events + PARTS)),
            dma((2, events)),
            dma((2, events)),
            dma,
            dma,
            dma,
            dma((2,)),
        ],
        compiler_params=pltpu.CompilerParams(
            collective_id=0, has_side_effects=True, vmem_limit_bytes=48 * 1024 * 1024
        ),
        cost_estimate=pl.CostEstimate(
            flops=4 * 3 * tl * tl * width + 4 * band * width * dout,
            bytes_accessed=2 * (3 * tl * width + rows * dout + band * dout),
            transcendentals=3 * tl * tl * heads,
        ),
    )(window_offsets.reshape(-1), queries.reshape(tl, width), kv, out_weight, gate)
    return mixed.reshape(1, 1, 1, 1, band, dout)


def solution(mesh):
    placed = (
        P("dp", "tm", None, None, None, "rows"),
        P("dp", "tm", None, None, None, None, "rows"),
        P("dp", "tm", None, None, None),
        P(("rows", "dp"), None),
        P("dp", None),
    )
    return jax.shard_map(
        local,
        mesh=mesh,
        in_specs=placed,
        out_specs=P("dp", "tm", None, None, "rows", None),
        check_vma=False,
    )
```

```python
import functools
import math

import jax
import jax.numpy as jnp
from jax import lax
from jax.experimental import pallas as pl
from jax.experimental.pallas import tpu as pltpu
from jax.sharding import PartitionSpec as P

HD = 128
MESH = pl.DeviceIdType.MESH
PLAN = {0: (1, 0), 1: (1, 1), 2: (2, 0), 3: (1, 0), 4: (1, 1), 5: (1, 0), 6: (1, 1)}


def kernel(
    ndp,
    ntm,
    heads,
    off_ref,
    q_ref,
    kv_in,
    w_ref,
    gate_ref,
    out_ref,
    kv_ref,
    a_buf,
    b_buf,
    wbuf,
    att,
    att_send,
    att_cut,
    total_ref,
    a_send,
    a_recv,
    b_send,
    b_recv,
    z_send,
    z_recv,
    c_send,
    c_recv,
    y_send,
    y_recv,
    d_send,
    d_recv,
    own_send,
    own_recv,
    own_local,
    att_sem,
):
    i = lax.axis_index("dp")
    t = lax.axis_index("tm")
    r = lax.axis_index("rows")
    other = 1 - r
    relay = ntm == 4
    odd = t % 2
    partner = t + 1 - 2 * odd
    beyond = t - 1 + 2 * odd
    has_b = jnp.logical_and(beyond >= 0, beyond < ntm)
    if relay:
        b_target = (t + 2) % 4
        b_sends = jnp.logical_not(has_b)
        greets_b = t >= 0
    else:
        b_target = jnp.clip(beyond, 0, ntm - 1)
        b_sends = has_b
        greets_b = has_b
    has_left = i > 0
    has_right = i < ndp - 1
    left = jnp.maximum(i - 1, 0)
    right = jnp.minimum(i + 1, ndp - 1)
    band = out_ref.shape[0]
    rows = w_ref.shape[0]
    steps = ndp - 1
    upper = t // 2
    if relay and rows % 192 == 0:
        edge, inner = rows // 6, rows // 3
        pieces = ((upper * (rows - edge), edge), (edge, inner), (edge + inner, inner))
        far_piece = ((1 - upper) * (rows - edge), edge)
        shared = True
    else:
        pieces = ((0, rows // 2), (rows // 2, rows // 2))
        far_piece = pieces[0]
        shared = False
    parts = len(pieces)

    def deinterleave(h):
        kv_ref[h] = jnp.swapaxes(kv_in[:, :, h * HD : (h + 1) * HD], 0, 1)

    barrier = pltpu.get_barrier_semaphore()

    def greet(device):
        pl.semaphore_signal(barrier, inc=1, device_id=device, device_id_type=MESH)

    greet({"rows": other})
    greet({"tm": partner})

    @pl.when(greets_b)
    def _():
        greet({"tm": b_target})

    @pl.when(has_left)
    def _():
        greet({"dp": left})

    @pl.when(has_right)
    def _():
        greet({"dp": right})

    for h in range(min(2, heads)):
        deinterleave(h)

    @pl.when(jnp.logical_not(has_b))
    def _():
        b_buf[...] = jnp.zeros_like(b_buf)

    peers = 2
    for present in (greets_b, has_left, has_right):
        peers = peers + jnp.where(present, 1, 0)
    pl.semaphore_wait(barrier, peers)

    def remote(src, dst, send, recv, device):
        return pltpu.make_async_remote_copy(
            src_ref=src, dst_ref=dst, send_sem=send, recv_sem=recv, device_id=device, device_id_type=MESH
        )

    def a_copy(h):
        return remote(kv_ref.at[h], a_buf.at[h], a_send.at[h], a_recv.at[h], {"tm": partner})

    def b_copy(h):
        src = a_buf if relay else kv_ref
        return remote(src.at[h], b_buf.at[h], b_send.at[h], b_recv.at[h], {"tm": b_target})

    def place(half, shard, spot):
        start = pl.multiple_of((half * ndp + shard) * rows + spot[0], 16)
        return wbuf.at[pl.ds(start, spot[1])]

    def own_piece(part):
        first, size = pieces[part]
        return w_ref.at[pl.ds(pl.multiple_of(first, 16), size)]

    def z_copy(src, shard, part, side, step):
        target = right if side == 0 else left
        return remote(
            src,
            place(r, shard, pieces[part]),
            z_send.at[side, step, part],
            z_recv.at[side, step, part],
            {"dp": target},
        )

    def c_copy(shard, part, side, step):
        spot = place(r, shard, pieces[part])
        return remote(
            spot, spot, c_send.at[side, step, part], c_recv.at[side, step, part], {"rows": other}
        )

    def y_copy(shard, side, step):
        spot = place(r, shard, pieces[0])
        return remote(
            spot, spot, y_send.at[side, step], y_recv.at[side, step], {"tm": b_target}
        )

    def d_copy(shard, side, step):
        spot = place(r, shard, far_piece)
        return remote(spot, spot, d_send.at[side, step], d_recv.at[side, step], {"rows": other})

    def shard_of(step, side):
        return i - 1 - step if side == 0 else i + 1 + step

    def valid(step, side):
        shard = shard_of(step, side)
        return shard >= 0 if side == 0 else shard < ndp

    sends_on = (has_right, has_left)

    for h in range(min(2, heads)):
        a_copy(h).start()
    for part in range(parts):
        for side in (0, 1):
            @pl.when(sends_on[side])
            def _():
                z_copy(own_piece(part), i, part, side, 0).start()
    own_spot = wbuf.at[pl.ds(pl.multiple_of((r * ndp + i) * rows, 16), rows)]
    own_copy = pltpu.make_async_copy(w_ref, own_spot, own_local)
    own_copy.start()
    own_across = remote(w_ref, own_spot, own_send, own_recv, {"rows": other})
    own_across.start()
    for h in range(2, heads):
        deinterleave(h)

    if not relay:
        @pl.when(b_sends)
        def _():
            for h in range(heads):
                b_copy(h).start()

    def weight_event(step, part):
        for side in (0, 1):
            @pl.when(valid(step, side))
            def _():
                shard = shard_of(step, side)
                spot = place(r, shard, pieces[part])
                z_copy(spot, shard, part, side, step).wait_recv()

                @pl.when(sends_on[side])
                def _():
                    z_copy(spot, shard, part, side, step + 1).start()

                if shared and part == 0:
                    y_copy(shard, side, step).start()
                c_copy(shard, part, side, step).start()

    def far_event(step):
        for side in (0, 1):
            @pl.when(valid(step, side))
            def _():
                shard = shard_of(step, side)
                y_copy(shard, side, step).wait_recv()
                d_copy(shard, side, step).start()

    def is_live(code):
        hit = off_ref[0] == code
        for k in range(1, off_ref.shape[0]):
            hit = jnp.logical_or(hit, off_ref[k] == code)
        return hit

    low = is_live(4)
    high = is_live(22)
    a_live = jnp.logical_or(jnp.logical_and(low, odd == 1), jnp.logical_and(high, odd == 0))
    b_live = jnp.logical_or(jnp.logical_and(low, odd == 0), jnp.logical_and(high, odd == 1))
    b_live = jnp.logical_and(b_live, has_b)
    dead = jnp.float32(-jnp.inf)
    a_bias = jnp.where(a_live, jnp.float32(0), dead)
    b_bias = jnp.where(b_live, jnp.float32(0), dead)
    factor = HD**-0.5 * math.log2(math.e)

    def score(q, keys):
        return lax.dot_general(
            q, keys, (((1,), (1,)), ((), ())), preferred_element_type=jnp.float32
        )

    def attend(h, which):
        q = q_ref[pl.ds(pl.multiple_of(which * band, 16), band), h * HD : (h + 1) * HD]
        parts = (
            score(q, kv_ref[h, 0]),
            score(q, a_buf[h, 0]) + a_bias,
            score(q, b_buf[h, 0]) + b_bias,
        )
        top = functools.reduce(
            jnp.maximum, [jnp.max(s, axis=1, keepdims=True) for s in parts]
        )
        total = 0.0
        acc = 0.0
        for s, held in zip(parts, (kv_ref, a_buf, b_buf)):
            p = jnp.exp2((s - top) * factor)
            total = total + jnp.sum(p, axis=1, keepdims=True)
            acc = acc + jnp.dot(
                p.astype(jnp.bfloat16), held[h, 1], preferred_element_type=jnp.float32
            )
        return (acc / total).astype(jnp.bfloat16)

    done = far_done = 0
    for h in range(heads + 1):
        if h < heads:
            a_copy(h).wait_recv()
            if h + 2 < heads:
                a_copy(h + 2).start()
            if relay:
                @pl.when(b_sends)
                def _():
                    b_copy(h).start()
        if ndp == 4:
            near, far = PLAN.get(h, (0, 0))
            for _ in range(near):
                weight_event(done // parts, done % parts)
                done += 1
            for _ in range(far if shared else 0):
                far_event(far_done)
                far_done += 1
        if h > 0:
            g = h - 1

            @pl.when(has_b)
            def _():
                b_copy(g).wait_recv()

            columns = pl.ds(g * HD, HD)
            att_send[:, columns] = attend(g, other)
            att[r, :, columns] = attend(g, r)

    across = remote(att_send, att.at[r], att_sem.at[0], att_sem.at[1], {"rows": other})
    across.start()

    own_copy.wait()
    own_across.wait_recv()
    across.wait_recv()
    for half in (0, 1):
        for shard in range(ndp):
            att_cut[half, shard] = att[half, :, shard * rows : (shard + 1) * rows]
    width = out_ref.shape[1]
    tile = 512 if width % 512 == 0 else width

    def product(shard, columns):
        halves = []
        for half in (0, 1):
            start = pl.multiple_of((half * ndp + shard) * rows, 16)
            halves.append(
                jnp.dot(
                    att_cut[half, shard],
                    wbuf[pl.ds(start, rows), columns],
                    preferred_element_type=jnp.float32,
                )
            )
        return halves[0] + halves[1]

    for start in range(0, width, tile):
        columns = pl.ds(start, tile)
        total_ref[:, columns] = product(i, columns)

    def arrive(step):
        for side in (0, 1):
            @pl.when(valid(step, side))
            def _():
                shard = shard_of(step, side)
                for part in range(parts):
                    c_copy(shard, part, side, step).wait_recv()
                if shared:
                    d_copy(shard, side, step).wait_recv()
                for start in range(0, width, tile):
                    columns = pl.ds(start, tile)
                    total_ref[:, columns] += product(shard, columns)

    if ndp == 4:
        for step in range(steps):
            for event in range(max(done, step * parts), (step + 1) * parts):
                weight_event(step, event % parts)
            if shared and far_done <= step:
                far_event(step)
            arrive(step)
    else:
        def advance(step, carry):
            for part in range(parts):
                weight_event(step, part)
            if shared:
                far_event(step)
            arrive(step)
            return carry

        lax.fori_loop(0, steps, advance, 0)

    out_ref[...] = (gate_ref[...] * total_ref[...]).astype(out_ref.dtype)

    for h in range(heads):
        a_copy(h).wait_send()

    @pl.when(b_sends)
    def _():
        for h in range(heads):
            b_copy(h).wait_send()

    own_across.wait_send()
    across.wait_send()

    for part in range(parts):
        for side in (0, 1):
            @pl.when(sends_on[side])
            def _():
                z_copy(own_piece(part), i, part, side, 0).wait_send()

    def sent(step, carry):
        for side in (0, 1):
            @pl.when(valid(step, side))
            def _():
                shard = shard_of(step, side)
                for part in range(parts):
                    c_copy(shard, part, side, step).wait_send()

                    @pl.when(sends_on[side])
                    def _():
                        spot = place(r, shard, pieces[part])
                        z_copy(spot, shard, part, side, step + 1).wait_send()

                if shared:
                    y_copy(shard, side, step).wait_send()
                    d_copy(shard, side, step).wait_send()
        return carry

    lax.fori_loop(0, steps, sent, 0)


def local(queries, keys_values, window_offsets, out_weight, gate):
    tl, width = queries.shape[4], queries.shape[5]
    heads = width // HD
    ndp, ntm, bands = lax.axis_size("dp"), lax.axis_size("tm"), lax.axis_size("rows")
    assert queries.shape[2] == queries.shape[3] == 1 and bands == 2 and ntm % 2 == 0
    band = tl // bands
    rows, dout = out_weight.shape
    kv = keys_values.reshape(tl, 2, width)
    bf16 = jnp.bfloat16
    vmem = pl.BlockSpec(memory_space=pltpu.VMEM)
    dma = pltpu.SemaphoreType.DMA
    mixed = pl.pallas_call(
        functools.partial(kernel, ndp, ntm, heads),
        out_shape=jax.ShapeDtypeStruct((band, dout), bf16),
        in_specs=[pl.BlockSpec(memory_space=pltpu.SMEM), vmem, vmem, vmem, vmem],
        out_specs=vmem,
        scratch_shapes=[
            pltpu.VMEM((heads, 2, tl, HD), bf16),
            pltpu.VMEM((heads, 2, tl, HD), bf16),
            pltpu.VMEM((heads, 2, tl, HD), bf16),
            pltpu.VMEM((2 * ndp * rows, dout), bf16),
            pltpu.VMEM((2, band, width), bf16),
            pltpu.VMEM((band, width), bf16),
            pltpu.VMEM((2, ndp, band, rows), bf16),
            pltpu.VMEM((band, dout), jnp.float32),
            dma((heads,)),
            dma((heads,)),
            dma((heads,)),
            dma((heads,)),
            dma((2, ndp, 3)),
            dma((2, ndp, 3)),
            dma((2, ndp, 3)),
            dma((2, ndp, 3)),
            dma((2, ndp)),
            dma((2, ndp)),
            dma((2, ndp)),
            dma((2, ndp)),
            dma,
            dma,
            dma,
            dma((2,)),
        ],
        compiler_params=pltpu.CompilerParams(
            collective_id=0, has_side_effects=True, vmem_limit_bytes=48 * 1024 * 1024
        ),
        cost_estimate=pl.CostEstimate(
            flops=4 * 3 * tl * tl * width + 4 * band * width * dout,
            bytes_accessed=2 * (3 * tl * width + rows * dout + band * dout),
            transcendentals=3 * tl * tl * heads,
        ),
    )(window_offsets.reshape(-1), queries.reshape(tl, width), kv, out_weight, gate)
    return mixed.reshape(1, 1, 1, 1, band, dout)


def solution(mesh):
    placed = (
        P("dp", "tm", None, None, None, "rows"),
        P("dp", "tm", None, None, None, None, "rows"),
        P("dp", "tm", None, None, None),
        P(("rows", "dp"), None),
        P("dp", None),
    )
    return jax.shard_map(
        local,
        mesh=mesh,
        in_specs=placed,
        out_specs=P("dp", "tm", None, None, "rows", None),
        check_vma=False,
    )
```

```python
import functools
import math

import jax
import jax.numpy as jnp
from jax import lax
from jax.experimental import pallas as pl
from jax.experimental.pallas import tpu as pltpu
from jax.sharding import PartitionSpec as P

HD = 128
MESH = pl.DeviceIdType.MESH
PLAN = {0: (1, 0), 1: (1, 0), 2: (2, 1), 3: (1, 0), 4: (1, 0), 5: (1, 1), 6: (1, 0)}
AHEAD = 3


def kernel(
    ndp,
    ntm,
    heads,
    off_hbm,
    q_hbm,
    kv_hbm,
    w_ref,
    gate_hbm,
    out_ref,
    off_ref,
    q_ref,
    kv_in,
    gate_ref,
    kv_ref,
    a_buf,
    b_buf,
    wbuf,
    att_own,
    att_other,
    att_cut,
    total_ref,
    a_send,
    a_recv,
    b_send,
    b_recv,
    z_send,
    z_recv,
    c_send,
    c_recv,
    y_send,
    y_recv,
    d_send,
    d_recv,
    own_send,
    own_recv,
    own_local,
    att_send,
    att_recv,
    in_sem,
):
    i = lax.axis_index("dp")
    t = lax.axis_index("tm")
    r = lax.axis_index("rows")
    other = 1 - r
    relay = ntm == 4
    odd = t % 2
    partner = t + 1 - 2 * odd
    beyond = t - 1 + 2 * odd
    has_b = jnp.logical_and(beyond >= 0, beyond < ntm)
    if relay:
        b_target = (t + 2) % 4
        b_sends = jnp.logical_not(has_b)
        greets_b = t >= 0
    else:
        b_target = jnp.clip(beyond, 0, ntm - 1)
        b_sends = has_b
        greets_b = has_b
    has_left = i > 0
    has_right = i < ndp - 1
    left = jnp.maximum(i - 1, 0)
    right = jnp.minimum(i + 1, ndp - 1)
    band = out_ref.shape[0]
    rows = w_ref.shape[0]
    steps = ndp - 1
    upper = t // 2
    if relay and rows % 192 == 0:
        edge, inner = rows // 6, rows // 3
        pieces = ((upper * (rows - edge), edge), (edge, inner), (edge + inner, inner))
        far_piece = ((1 - upper) * (rows - edge), edge)
        shared = True
    else:
        pieces = ((0, rows // 2), (rows // 2, rows // 2))
        far_piece = pieces[0]
        shared = False
    parts = len(pieces)

    def deinterleave(h):
        kv_ref[h] = jnp.swapaxes(kv_in[:, :, h * HD : (h + 1) * HD], 0, 1)

    loads = [
        pltpu.make_async_copy(src, dst, in_sem.at[k])
        for k, (src, dst) in enumerate(
            ((kv_hbm, kv_in), (q_hbm, q_ref), (gate_hbm, gate_ref), (off_hbm, off_ref))
        )
    ]
    for load in loads:
        load.start()

    barrier = pltpu.get_barrier_semaphore()

    def greet(device):
        pl.semaphore_signal(barrier, inc=1, device_id=device, device_id_type=MESH)

    greet({"rows": other})
    greet({"tm": partner})

    @pl.when(greets_b)
    def _():
        greet({"tm": b_target})

    @pl.when(has_left)
    def _():
        greet({"dp": left})

    @pl.when(has_right)
    def _():
        greet({"dp": right})

    loads[0].wait()
    for h in range(min(AHEAD, heads)):
        deinterleave(h)

    @pl.when(jnp.logical_not(has_b))
    def _():
        b_buf[...] = jnp.zeros_like(b_buf)

    peers = 2
    for present in (greets_b, has_left, has_right):
        peers = peers + jnp.where(present, 1, 0)
    pl.semaphore_wait(barrier, peers)

    def remote(src, dst, send, recv, device):
        return pltpu.make_async_remote_copy(
            src_ref=src, dst_ref=dst, send_sem=send, recv_sem=recv, device_id=device, device_id_type=MESH
        )

    def a_copy(h, s):
        return remote(
            kv_ref.at[h, s], a_buf.at[h, s], a_send.at[h, s], a_recv.at[h, s], {"tm": partner}
        )

    def b_copy(h, s):
        src = a_buf if relay else kv_ref
        return remote(
            src.at[h, s], b_buf.at[h, s], b_send.at[h, s], b_recv.at[h, s], {"tm": b_target}
        )

    def across(h):
        theirs = pl.ds(pl.multiple_of(other * band, 16), band)
        return remote(
            att_own.at[h, theirs], att_other.at[h], att_send.at[h], att_recv.at[h], {"rows": other}
        )

    def place(half, shard, spot):
        start = pl.multiple_of((half * ndp + shard) * rows + spot[0], 16)
        return wbuf.at[pl.ds(start, spot[1])]

    def own_piece(part):
        first, size = pieces[part]
        return w_ref.at[pl.ds(pl.multiple_of(first, 16), size)]

    def z_copy(src, shard, part, side, step):
        target = right if side == 0 else left
        return remote(
            src,
            place(r, shard, pieces[part]),
            z_send.at[side, step, part],
            z_recv.at[side, step, part],
            {"dp": target},
        )

    def c_copy(shard, part, side, step):
        spot = place(r, shard, pieces[part])
        return remote(
            spot, spot, c_send.at[side, step, part], c_recv.at[side, step, part], {"rows": other}
        )

    def y_copy(shard, side, step):
        spot = place(r, shard, pieces[0])
        return remote(
            spot, spot, y_send.at[side, step], y_recv.at[side, step], {"tm": b_target}
        )

    def d_copy(shard, side, step):
        spot = place(r, shard, far_piece)
        return remote(spot, spot, d_send.at[side, step], d_recv.at[side, step], {"rows": other})

    def shard_of(step, side):
        return i - 1 - step if side == 0 else i + 1 + step

    def valid(step, side):
        shard = shard_of(step, side)
        return shard >= 0 if side == 0 else shard < ndp

    sends_on = (has_right, has_left)

    for h in range(min(AHEAD, heads)):
        for s in (0, 1):
            a_copy(h, s).start()
    for part in range(parts):
        for side in (0, 1):
            @pl.when(sends_on[side])
            def _():
                z_copy(own_piece(part), i, part, side, 0).start()
    own_spot = wbuf.at[pl.ds(pl.multiple_of((r * ndp + i) * rows, 16), rows)]
    own_copy = pltpu.make_async_copy(w_ref, own_spot, own_local)
    own_copy.start()
    own_across = remote(w_ref, own_spot, own_send, own_recv, {"rows": other})
    own_across.start()
    for h in range(AHEAD, heads):
        deinterleave(h)

    if not relay:
        @pl.when(b_sends)
        def _():
            for h in range(heads):
                for s in (0, 1):
                    b_copy(h, s).start()

    def weight_event(step, part):
        for side in (0, 1):
            @pl.when(valid(step, side))
            def _():
                shard = shard_of(step, side)
                spot = place(r, shard, pieces[part])
                z_copy(spot, shard, part, side, step).wait_recv()

                @pl.when(sends_on[side])
                def _():
                    z_copy(spot, shard, part, side, step + 1).start()

                if shared and part == 0:
                    y_copy(shard, side, step).start()
                c_copy(shard, part, side, step).start()

    def far_event(step):
        for side in (0, 1):
            @pl.when(valid(step, side))
            def _():
                shard = shard_of(step, side)
                y_copy(shard, side, step).wait_recv()
                d_copy(shard, side, step).start()

    for load in loads[1:]:
        load.wait()

    def is_live(code):
        hit = off_ref[0] == code
        for k in range(1, off_ref.shape[0]):
            hit = jnp.logical_or(hit, off_ref[k] == code)
        return hit

    low = is_live(4)
    high = is_live(22)
    a_live = jnp.logical_or(jnp.logical_and(low, odd == 1), jnp.logical_and(high, odd == 0))
    b_live = jnp.logical_or(jnp.logical_and(low, odd == 0), jnp.logical_and(high, odd == 1))
    b_live = jnp.logical_and(b_live, has_b)
    dead = jnp.float32(-jnp.inf)
    a_bias = jnp.where(a_live, jnp.float32(0), dead)
    b_bias = jnp.where(b_live, jnp.float32(0), dead)
    factor = HD**-0.5 * math.log2(math.e)

    def score(q, keys):
        return lax.dot_general(
            q, keys, (((1,), (1,)), ((), ())), preferred_element_type=jnp.float32
        )

    def attend(h):
        q = q_ref[:, h * HD : (h + 1) * HD]
        held = (kv_ref, a_buf, b_buf)
        biases = (jnp.float32(0), a_bias, b_bias)
        scores = [score(q, buf[h, 0]) for buf in held]
        top = functools.reduce(
            jnp.maximum,
            [jnp.max(s, axis=1, keepdims=True) + bias for s, bias in zip(scores, biases)],
        )
        top = top * factor
        ones = jnp.ones((kv_in.shape[0], HD), jnp.bfloat16)
        acc = 0.0
        for s, bias, buf in zip(scores, biases, held):
            p = jnp.exp2(s * factor - (top - bias)).astype(jnp.bfloat16)
            values = jnp.concatenate([buf[h, 1], ones], axis=1)
            acc = acc + jnp.dot(p, values, preferred_element_type=jnp.float32)
        att_own[h] = (acc[:, :HD] / acc[:, HD:]).astype(jnp.bfloat16)
        across(h).start()

    done = far_done = 0
    for h in range(heads + 2):
        if h < heads:
            for s in (0, 1):
                a_copy(h, s).wait_recv()
                if relay:
                    @pl.when(b_sends)
                    def _():
                        b_copy(h, s).start()
                if h + AHEAD < heads:
                    a_copy(h + AHEAD, s).start()
        if ndp == 4:
            near, far = PLAN.get(h, (0, 0))
            for _ in range(near):
                weight_event(done // parts, done % parts)
                done += 1
            for _ in range(far if shared else 0):
                far_event(far_done)
                far_done += 1
        if h > 1:
            g = h - 2

            @pl.when(has_b)
            def _():
                for s in (0, 1):
                    b_copy(g, s).wait_recv()

            attend(g)

    own_copy.wait()
    own_across.wait_recv()
    for h in range(heads):
        across(h).wait_recv()
    mine = pl.ds(pl.multiple_of(r * band, 16), band)
    own_half = jnp.concatenate([att_own[h, mine] for h in range(heads)], axis=1)
    other_half = jnp.concatenate([att_other[h] for h in range(heads)], axis=1)
    for shard in range(ndp):
        columns = slice(shard * rows, (shard + 1) * rows)
        att_cut[r, shard] = own_half[:, columns]
        att_cut[other, shard] = other_half[:, columns]
    width = out_ref.shape[1]
    tile = 512 if width % 512 == 0 else width

    def product(shard, columns):
        halves = []
        for half in (0, 1):
            start = pl.multiple_of((half * ndp + shard) * rows, 16)
            halves.append(
                jnp.dot(
                    att_cut[half, shard],
                    wbuf[pl.ds(start, rows), columns],
                    preferred_element_type=jnp.float32,
                )
            )
        return halves[0] + halves[1]

    for start in range(0, width, tile):
        columns = pl.ds(start, tile)
        total_ref[:, columns] = product(i, columns)

    def arrive(step):
        for side in (0, 1):
            @pl.when(valid(step, side))
            def _():
                shard = shard_of(step, side)
                for part in range(parts):
                    c_copy(shard, part, side, step).wait_recv()
                if shared:
                    d_copy(shard, side, step).wait_recv()
                for start in range(0, width, tile):
                    columns = pl.ds(start, tile)
                    total_ref[:, columns] += product(shard, columns)

    if ndp == 4:
        for step in range(steps):
            for event in range(max(done, step * parts), (step + 1) * parts):
                weight_event(step, event % parts)
            if shared and far_done <= step:
                far_event(step)
            arrive(step)
    else:
        def advance(step, carry):
            for part in range(parts):
                weight_event(step, part)
            if shared:
                far_event(step)
            arrive(step)
            return carry

        lax.fori_loop(0, steps, advance, 0)

    out_ref[...] = (gate_ref[...] * total_ref[...]).astype(out_ref.dtype)

    for h in range(heads):
        across(h).wait_send()
        for s in (0, 1):
            a_copy(h, s).wait_send()

    @pl.when(b_sends)
    def _():
        for h in range(heads):
            for s in (0, 1):
                b_copy(h, s).wait_send()

    own_across.wait_send()

    for part in range(parts):
        for side in (0, 1):
            @pl.when(sends_on[side])
            def _():
                z_copy(own_piece(part), i, part, side, 0).wait_send()

    def sent(step, carry):
        for side in (0, 1):
            @pl.when(valid(step, side))
            def _():
                shard = shard_of(step, side)
                for part in range(parts):
                    c_copy(shard, part, side, step).wait_send()

                    @pl.when(sends_on[side])
                    def _():
                        spot = place(r, shard, pieces[part])
                        z_copy(spot, shard, part, side, step + 1).wait_send()

                if shared:
                    y_copy(shard, side, step).wait_send()
                    d_copy(shard, side, step).wait_send()
        return carry

    lax.fori_loop(0, steps, sent, 0)


def local(queries, keys_values, window_offsets, out_weight, gate):
    tl, width = queries.shape[4], queries.shape[5]
    heads = width // HD
    ndp, ntm, bands = lax.axis_size("dp"), lax.axis_size("tm"), lax.axis_size("rows")
    assert queries.shape[2] == queries.shape[3] == 1 and bands == 2 and ntm % 2 == 0
    band = tl // bands
    rows, dout = out_weight.shape
    kv = keys_values.reshape(tl, 2, width)
    bf16 = jnp.bfloat16
    vmem = pl.BlockSpec(memory_space=pltpu.VMEM)
    hbm = pl.BlockSpec(memory_space=pltpu.HBM)
    dma = pltpu.SemaphoreType.DMA
    mixed = pl.pallas_call(
        functools.partial(kernel, ndp, ntm, heads),
        out_shape=jax.ShapeDtypeStruct((band, dout), bf16),
        in_specs=[hbm] * 5,
        out_specs=vmem,
        scratch_shapes=[
            pltpu.SMEM((window_offsets.size,), jnp.int32),
            pltpu.VMEM((tl, width), bf16),
            pltpu.VMEM((tl, 2, width), bf16),
            pltpu.VMEM((1, dout), jnp.float32),
            pltpu.VMEM((heads, 2, tl, HD), bf16),
            pltpu.VMEM((heads, 2, tl, HD), bf16),
            pltpu.VMEM((heads, 2, tl, HD), bf16),
            pltpu.VMEM((2 * ndp * rows, dout), bf16),
            pltpu.VMEM((heads, tl, HD), bf16),
            pltpu.VMEM((heads, band, HD), bf16),
            pltpu.VMEM((2, ndp, band, rows), bf16),
            pltpu.VMEM((band, dout), jnp.float32),
            dma((heads, 2)),
            dma((heads, 2)),
            dma((heads, 2)),
            dma((heads, 2)),
            dma((2, ndp, 3)),
            dma((2, ndp, 3)),
            dma((2, ndp, 3)),
            dma((2, ndp, 3)),
            dma((2, ndp)),
            dma((2, ndp)),
            dma((2, ndp)),
            dma((2, ndp)),
            dma,
            dma,
            dma,
            dma((heads,)),
            dma((heads,)),
            dma((4,)),
        ],
        compiler_params=pltpu.CompilerParams(
            collective_id=0, has_side_effects=True, vmem_limit_bytes=64 * 1024 * 1024
        ),
        cost_estimate=pl.CostEstimate(
            flops=4 * 3 * tl * tl * width + 4 * band * width * dout,
            bytes_accessed=2 * (3 * tl * width + rows * dout + band * dout),
            transcendentals=3 * tl * tl * heads,
        ),
    )(window_offsets.reshape(-1), queries.reshape(tl, width), kv, out_weight, gate)
    return mixed.reshape(1, 1, 1, 1, band, dout)


def solution(mesh):
    placed = (
        P("dp", "tm", None, None, None, "rows"),
        P("dp", "tm", None, None, None, None, "rows"),
        P("dp", "tm", None, None, None),
        P(("rows", "dp"), None),
        P("dp", None),
    )
    return jax.shard_map(
        local,
        mesh=mesh,
        in_specs=placed,
        out_specs=P("dp", "tm", None, None, "rows", None),
        check_vma=False,
    )
```

```python
import functools
import math

import jax
import jax.numpy as jnp
from jax import lax
from jax.experimental import pallas as pl
from jax.experimental.pallas import tpu as pltpu
from jax.sharding import PartitionSpec as P

HD = 128
MESH = pl.DeviceIdType.MESH
PLAN = {0: 1, 1: 1, 2: 2, 3: 1, 4: 1, 5: 1, 6: 1}
AHEAD = 3


def kernel(
    ndp,
    ntm,
    heads,
    off_hbm,
    q_hbm,
    kv_hbm,
    w_ref,
    gate_hbm,
    out_ref,
    off_ref,
    q_ref,
    kv_in,
    gate_ref,
    kv_ref,
    a_buf,
    b_buf,
    wbuf,
    att_own,
    att_other,
    total_ref,
    a_send,
    a_recv,
    b_send,
    b_recv,
    z_send,
    z_recv,
    c_send,
    c_recv,
    y_send,
    y_recv,
    d_send,
    d_recv,
    own_send,
    own_recv,
    own_local,
    att_send,
    att_recv,
    in_sem,
):
    i = lax.axis_index("dp")
    t = lax.axis_index("tm")
    r = lax.axis_index("rows")
    other = 1 - r
    relay = ntm == 4
    odd = t % 2
    partner = t + 1 - 2 * odd
    beyond = t - 1 + 2 * odd
    has_b = jnp.logical_and(beyond >= 0, beyond < ntm)
    if relay:
        b_target = (t + 2) % 4
        b_sends = jnp.logical_not(has_b)
        greets_b = t >= 0
    else:
        b_target = jnp.clip(beyond, 0, ntm - 1)
        b_sends = has_b
        greets_b = has_b
    has_left = i > 0
    has_right = i < ndp - 1
    left = jnp.maximum(i - 1, 0)
    right = jnp.minimum(i + 1, ndp - 1)
    band = out_ref.shape[0]
    rows = w_ref.shape[0]
    steps = ndp - 1
    upper = t // 2
    if relay and ndp == 4 and heads == 6 and rows == 192:
        edge, inner = rows // 6, rows // 3
        pieces = ((upper * (rows - edge), edge), (edge, inner), (edge + inner, inner))
        far_piece = ((1 - upper) * (rows - edge), edge)
        shared = True
    else:
        pieces = ((0, rows // 2), (rows // 2, rows // 2))
        far_piece = pieces[0]
        shared = False
    parts = len(pieces)

    descending = jnp.where(i >= ndp // 2, 1, 0)

    def head(g):
        return g + descending * (heads - 1 - 2 * g)

    def lanes(g):
        return pl.ds(pl.multiple_of(head(g) * HD, HD), HD)

    def deinterleave(g):
        kv_ref[head(g)] = jnp.swapaxes(kv_in[:, :, lanes(g)], 0, 1)

    loads = [
        pltpu.make_async_copy(src, dst, in_sem.at[k])
        for k, (src, dst) in enumerate(
            ((kv_hbm, kv_in), (q_hbm, q_ref), (gate_hbm, gate_ref), (off_hbm, off_ref))
        )
    ]
    for load in loads:
        load.start()

    barrier = pltpu.get_barrier_semaphore()

    def greet(device):
        pl.semaphore_signal(barrier, inc=1, device_id=device, device_id_type=MESH)

    greet({"rows": other})
    greet({"tm": partner})

    @pl.when(greets_b)
    def _():
        greet({"tm": b_target})

    @pl.when(has_left)
    def _():
        greet({"dp": left})

    @pl.when(has_right)
    def _():
        greet({"dp": right})

    loads[0].wait()
    for h in range(min(AHEAD, heads)):
        deinterleave(h)

    @pl.when(jnp.logical_not(has_b))
    def _():
        b_buf[...] = jnp.zeros_like(b_buf)

    peers = 2
    for present in (greets_b, has_left, has_right):
        peers = peers + jnp.where(present, 1, 0)
    pl.semaphore_wait(barrier, peers)

    def remote(src, dst, send, recv, device):
        return pltpu.make_async_remote_copy(
            src_ref=src, dst_ref=dst, send_sem=send, recv_sem=recv, device_id=device, device_id_type=MESH
        )

    def a_copy(g, s):
        h = head(g)
        return remote(
            kv_ref.at[h, s], a_buf.at[h, s], a_send.at[g, s], a_recv.at[g, s], {"tm": partner}
        )

    def b_copy(g, s):
        h = head(g)
        src = a_buf if relay else kv_ref
        return remote(
            src.at[h, s], b_buf.at[h, s], b_send.at[g, s], b_recv.at[g, s], {"tm": b_target}
        )

    def across(g):
        h = head(g)
        theirs = pl.ds(pl.multiple_of(other * band, 16), band)
        return remote(
            att_own.at[h, theirs], att_other.at[h], att_send.at[g], att_recv.at[g], {"rows": other}
        )

    def place(half, shard, spot):
        start = pl.multiple_of((half * ndp + shard) * rows + spot[0], 16)
        return wbuf.at[pl.ds(start, spot[1])]

    def own_piece(part):
        first, size = pieces[part]
        return w_ref.at[pl.ds(pl.multiple_of(first, 16), size)]

    def z_copy(src, shard, part, side, step):
        target = right if side == 0 else left
        return remote(
            src,
            place(r, shard, pieces[part]),
            z_send.at[side, step, part],
            z_recv.at[side, step, part],
            {"dp": target},
        )

    def c_copy(shard, part, side, step):
        spot = place(r, shard, pieces[part])
        return remote(
            spot, spot, c_send.at[side, step, part], c_recv.at[side, step, part], {"rows": other}
        )

    def y_copy(shard, side, step):
        spot = place(r, shard, pieces[0])
        return remote(
            spot, spot, y_send.at[side, step], y_recv.at[side, step], {"tm": b_target}
        )

    def d_copy(shard, side, step):
        spot = place(r, shard, far_piece)
        return remote(spot, spot, d_send.at[side, step], d_recv.at[side, step], {"rows": other})

    def shard_of(step, side):
        return i - 1 - step if side == 0 else i + 1 + step

    def valid(step, side):
        shard = shard_of(step, side)
        return shard >= 0 if side == 0 else shard < ndp

    sends_on = (has_right, has_left)

    for h in range(min(AHEAD, heads)):
        for s in (0, 1):
            a_copy(h, s).start()
    for part in range(parts):
        for side in (0, 1):
            @pl.when(sends_on[side])
            def _():
                z_copy(own_piece(part), i, part, side, 0).start()
    own_spot = wbuf.at[pl.ds(pl.multiple_of((r * ndp + i) * rows, 16), rows)]
    own_copy = pltpu.make_async_copy(w_ref, own_spot, own_local)
    own_copy.start()
    own_across = remote(w_ref, own_spot, own_send, own_recv, {"rows": other})
    own_across.start()
    for h in range(AHEAD, heads):
        deinterleave(h)

    if not relay:
        @pl.when(b_sends)
        def _():
            for h in range(heads):
                for s in (0, 1):
                    b_copy(h, s).start()

    def weight_event(step, part):
        for side in (0, 1):
            @pl.when(valid(step, side))
            def _():
                shard = shard_of(step, side)
                spot = place(r, shard, pieces[part])
                z_copy(spot, shard, part, side, step).wait_recv()

                @pl.when(sends_on[side])
                def _():
                    z_copy(spot, shard, part, side, step + 1).start()

                if shared and part == 0 and step == 0:
                    y_copy(shard, side, step).start()
                c_copy(shard, part, side, step).start()

    def relay_edge(step):
        for side in (0, 1):
            @pl.when(valid(step, side))
            def _():
                y_copy(shard_of(step, side), side, step).start()

    def far_event(step):
        for side in (0, 1):
            @pl.when(valid(step, side))
            def _():
                shard = shard_of(step, side)
                y_copy(shard, side, step).wait_recv()
                d_copy(shard, side, step).start()

    for load in loads[1:]:
        load.wait()

    def is_live(code):
        hit = off_ref[0] == code
        for k in range(1, off_ref.shape[0]):
            hit = jnp.logical_or(hit, off_ref[k] == code)
        return hit

    low = is_live(4)
    high = is_live(22)
    a_live = jnp.logical_or(jnp.logical_and(low, odd == 1), jnp.logical_and(high, odd == 0))
    b_live = jnp.logical_or(jnp.logical_and(low, odd == 0), jnp.logical_and(high, odd == 1))
    b_live = jnp.logical_and(b_live, has_b)
    dead = jnp.float32(-jnp.inf)
    a_bias = jnp.where(a_live, jnp.float32(0), dead)
    b_bias = jnp.where(b_live, jnp.float32(0), dead)
    factor = HD**-0.5 * math.log2(math.e)

    def score(q, keys):
        return lax.dot_general(
            q, keys, (((1,), (1,)), ((), ())), preferred_element_type=jnp.float32
        )

    def attend(g):
        h = head(g)
        q = q_ref[:, lanes(g)]
        held = (kv_ref, a_buf, b_buf)
        biases = (jnp.float32(0), a_bias, b_bias)
        scores = [score(q, buf[h, 0]) for buf in held]
        top = functools.reduce(
            jnp.maximum,
            [jnp.max(s, axis=1, keepdims=True) + bias for s, bias in zip(scores, biases)],
        )
        top = top * factor
        ones = jnp.ones((kv_in.shape[0], HD), jnp.bfloat16)
        acc = 0.0
        for s, bias, buf in zip(scores, biases, held):
            p = jnp.exp2(s * factor - (top - bias)).astype(jnp.bfloat16)
            values = jnp.concatenate([buf[h, 1], ones], axis=1)
            acc = acc + jnp.dot(p, values, preferred_element_type=jnp.float32)
        att_own[h] = (acc[:, :HD] / acc[:, HD:]).astype(jnp.bfloat16)
        across(g).start()

    width = out_ref.shape[1]
    tile = 512 if width % 512 == 0 else width
    mine = pl.ds(pl.multiple_of(r * band, 16), band)

    def project(p):
        first = p + descending * (heads // 2 - 1 - 2 * p)
        for g in (2 * p, 2 * p + 1):
            across(g).wait_recv()
        own = jnp.concatenate([att_own[2 * first + k, mine] for k in (0, 1)], axis=1)
        their = jnp.concatenate([att_other[2 * first + k] for k in (0, 1)], axis=1)
        for start in range(0, width, tile):
            columns = pl.ds(start, tile)
            value = 0.0
            for half, part in ((r, own), (other, their)):
                begin = pl.multiple_of(half * ndp * rows + first * 2 * HD, 2 * HD)
                value += jnp.dot(
                    part, wbuf[pl.ds(begin, 2 * HD), columns], preferred_element_type=jnp.float32
                )
            if p == 0:
                total_ref[:, columns] = value
            elif p < heads // 2 - 1:
                total_ref[:, columns] += value
            else:
                value = gate_ref[:, columns] * (total_ref[:, columns] + value)
                out_ref[:, columns] = value.astype(out_ref.dtype)

    def arrive(step):
        for side in (0, 1):
            @pl.when(valid(step, side))
            def _():
                shard = shard_of(step, side)
                for part in range(parts):
                    c_copy(shard, part, side, step).wait_recv()
                if shared:
                    d_copy(shard, side, step).wait_recv()

    staged = shared
    done = 0
    for h in range(heads + 1):
        if h < heads:
            for s in (0, 1):
                a_copy(h, s).wait_recv()
                if relay:
                    @pl.when(b_sends)
                    def _():
                        b_copy(h, s).start()
                if h + AHEAD < heads:
                    a_copy(h + AHEAD, s).start()
        if staged:
            for _ in range(PLAN.get(h, 0)):
                weight_event(done // parts, done % parts)
                done += 1
            if h == 2:
                far_event(0)
            if h == 5:
                relay_edge(1)
                relay_edge(2)
        if h > 0:
            g = h - 1

            @pl.when(has_b)
            def _():
                for s in (0, 1):
                    b_copy(g, s).wait_recv()

            attend(g)
            if staged and g == 3:
                own_copy.wait()
                own_across.wait_recv()
                arrive(0)
                project(0)

    if staged:
        far_event(1)
        weight_event(2, 2)
        arrive(1)
        project(1)
        far_event(2)
        arrive(2)
        project(2)
    else:
        def advance(step, carry):
            for part in range(parts):
                weight_event(step, part)
            return carry

        lax.fori_loop(0, steps, advance, 0)
        own_copy.wait()
        own_across.wait_recv()
        lax.fori_loop(0, steps, lambda step, carry: (arrive(step), carry)[1], 0)
        for p in range(heads // 2):
            project(p)

    for h in range(heads):
        across(h).wait_send()
        for s in (0, 1):
            a_copy(h, s).wait_send()

    @pl.when(b_sends)
    def _():
        for h in range(heads):
            for s in (0, 1):
                b_copy(h, s).wait_send()

    own_across.wait_send()

    for part in range(parts):
        for side in (0, 1):
            @pl.when(sends_on[side])
            def _():
                z_copy(own_piece(part), i, part, side, 0).wait_send()

    def sent(step, carry):
        for side in (0, 1):
            @pl.when(valid(step, side))
            def _():
                shard = shard_of(step, side)
                for part in range(parts):
                    c_copy(shard, part, side, step).wait_send()

                    @pl.when(sends_on[side])
                    def _():
                        spot = place(r, shard, pieces[part])
                        z_copy(spot, shard, part, side, step + 1).wait_send()

                if shared:
                    y_copy(shard, side, step).wait_send()
                    d_copy(shard, side, step).wait_send()
        return carry

    lax.fori_loop(0, steps, sent, 0)


def local(queries, keys_values, window_offsets, out_weight, gate):
    tl, width = queries.shape[4], queries.shape[5]
    heads = width // HD
    ndp, ntm, bands = lax.axis_size("dp"), lax.axis_size("tm"), lax.axis_size("rows")
    assert queries.shape[2] == queries.shape[3] == 1 and bands == 2 and ntm % 2 == 0 and heads % 2 == 0
    band = tl // bands
    rows, dout = out_weight.shape
    kv = keys_values.reshape(tl, 2, width)
    bf16 = jnp.bfloat16
    vmem = pl.BlockSpec(memory_space=pltpu.VMEM)
    hbm = pl.BlockSpec(memory_space=pltpu.HBM)
    dma = pltpu.SemaphoreType.DMA
    mixed = pl.pallas_call(
        functools.partial(kernel, ndp, ntm, heads),
        out_shape=jax.ShapeDtypeStruct((band, dout), bf16),
        in_specs=[hbm] * 5,
        out_specs=vmem,
        scratch_shapes=[
            pltpu.SMEM((window_offsets.size,), jnp.int32),
            pltpu.VMEM((tl, width), bf16),
            pltpu.VMEM((tl, 2, width), bf16),
            pltpu.VMEM((1, dout), jnp.float32),
            pltpu.VMEM((heads, 2, tl, HD), bf16),
            pltpu.VMEM((heads, 2, tl, HD), bf16),
            pltpu.VMEM((heads, 2, tl, HD), bf16),
            pltpu.VMEM((2 * ndp * rows, dout), bf16),
            pltpu.VMEM((heads, tl, HD), bf16),
            pltpu.VMEM((heads, band, HD), bf16),
            pltpu.VMEM((band, dout), jnp.float32),
            dma((heads, 2)),
            dma((heads, 2)),
            dma((heads, 2)),
            dma((heads, 2)),
            dma((2, ndp, 3)),
            dma((2, ndp, 3)),
            dma((2, ndp, 3)),
            dma((2, ndp, 3)),
            dma((2, ndp)),
            dma((2, ndp)),
            dma((2, ndp)),
            dma((2, ndp)),
            dma,
            dma,
            dma,
            dma((heads,)),
            dma((heads,)),
            dma((4,)),
        ],
        compiler_params=pltpu.CompilerParams(
            collective_id=0, has_side_effects=True, vmem_limit_bytes=64 * 1024 * 1024
        ),
        cost_estimate=pl.CostEstimate(
            flops=4 * 3 * tl * tl * width + 4 * band * width * dout,
            bytes_accessed=2 * (3 * tl * width + rows * dout + band * dout),
            transcendentals=3 * tl * tl * heads,
        ),
    )(window_offsets.reshape(-1), queries.reshape(tl, width), kv, out_weight, gate)
    return mixed.reshape(1, 1, 1, 1, band, dout)


def solution(mesh):
    placed = (
        P("dp", "tm", None, None, None, "rows"),
        P("dp", "tm", None, None, None, None, "rows"),
        P("dp", "tm", None, None, None),
        P(("rows", "dp"), None),
        P("dp", None),
    )
    return jax.shard_map(
        local,
        mesh=mesh,
        in_specs=placed,
        out_specs=P("dp", "tm", None, None, "rows", None),
        check_vma=False,
    )
```

```python
import functools
import math

import jax
import jax.numpy as jnp
from jax import lax
from jax.experimental import pallas as pl
from jax.experimental.pallas import tpu as pltpu
from jax.sharding import PartitionSpec as P

HD = 128
MESH = pl.DeviceIdType.MESH
PLAN = {0: 1, 1: 1, 2: 2, 3: 1, 4: 1, 5: 1, 6: 1}
AHEAD = 3


def kernel(
    ndp,
    ntm,
    heads,
    off_hbm,
    q_hbm,
    kv_hbm,
    w_ref,
    gate_hbm,
    out_ref,
    off_ref,
    q_ref,
    kv_in,
    gate_ref,
    kv_ref,
    a_buf,
    b_buf,
    wbuf,
    att_own,
    att_other,
    total_ref,
    a_send,
    a_recv,
    b_send,
    b_recv,
    z_send,
    z_recv,
    c_send,
    c_recv,
    y_send,
    y_recv,
    d_send,
    d_recv,
    own_send,
    own_recv,
    own_local,
    att_send,
    att_recv,
    in_sem,
):
    i = lax.axis_index("dp")
    t = lax.axis_index("tm")
    r = lax.axis_index("rows")
    other = 1 - r
    relay = ntm == 4
    odd = t % 2
    partner = t + 1 - 2 * odd
    beyond = t - 1 + 2 * odd
    has_b = jnp.logical_and(beyond >= 0, beyond < ntm)
    if relay:
        b_target = (t + 2) % 4
        b_sends = jnp.logical_not(has_b)
        greets_b = t >= 0
    else:
        b_target = jnp.clip(beyond, 0, ntm - 1)
        b_sends = has_b
        greets_b = has_b
    has_left = i > 0
    has_right = i < ndp - 1
    left = jnp.maximum(i - 1, 0)
    right = jnp.minimum(i + 1, ndp - 1)
    band = out_ref.shape[0]
    rows = w_ref.shape[0]
    steps = ndp - 1
    upper = t // 2
    if relay and ndp == 4 and heads == 6 and rows == 192:
        edge, inner = rows // 6, rows // 3
        pieces = ((upper * (rows - edge), edge), (edge, inner), (edge + inner, inner))
        far_piece = ((1 - upper) * (rows - edge), edge)
        shared = True
    else:
        pieces = ((0, rows // 2), (rows // 2, rows // 2))
        far_piece = pieces[0]
        shared = False
    parts = len(pieces)

    descending = jnp.where(i >= ndp // 2, 1, 0)

    def head(g):
        return g + descending * (heads - 1 - 2 * g)

    def lanes(g):
        return pl.ds(pl.multiple_of(head(g) * HD, HD), HD)

    def deinterleave(g):
        kv_ref[head(g)] = jnp.swapaxes(kv_in[:, :, lanes(g)], 0, 1)

    loads = [
        pltpu.make_async_copy(src, dst, in_sem.at[k])
        for k, (src, dst) in enumerate(
            ((kv_hbm, kv_in), (q_hbm, q_ref), (gate_hbm, gate_ref), (off_hbm, off_ref))
        )
    ]
    for load in loads:
        load.start()

    barrier = pltpu.get_barrier_semaphore()

    def greet(device):
        pl.semaphore_signal(barrier, inc=1, device_id=device, device_id_type=MESH)

    greet({"rows": other})
    greet({"tm": partner})

    @pl.when(greets_b)
    def _():
        greet({"tm": b_target})

    @pl.when(has_left)
    def _():
        greet({"dp": left})

    @pl.when(has_right)
    def _():
        greet({"dp": right})

    peers = 2
    for present in (greets_b, has_left, has_right):
        peers = peers + jnp.where(present, 1, 0)
    pl.semaphore_wait(barrier, peers)

    def remote(src, dst, send, recv, device):
        return pltpu.make_async_remote_copy(
            src_ref=src, dst_ref=dst, send_sem=send, recv_sem=recv, device_id=device, device_id_type=MESH
        )

    def a_copy(g, s):
        h = head(g)
        return remote(
            kv_ref.at[h, s], a_buf.at[h, s], a_send.at[g, s], a_recv.at[g, s], {"tm": partner}
        )

    def b_copy(g, s):
        h = head(g)
        src = a_buf if relay else kv_ref
        return remote(
            src.at[h, s], b_buf.at[h, s], b_send.at[g, s], b_recv.at[g, s], {"tm": b_target}
        )

    def across(g):
        h = head(g)
        theirs = pl.ds(pl.multiple_of(other * band, 16), band)
        return remote(
            att_own.at[h, theirs], att_other.at[h], att_send.at[g], att_recv.at[g], {"rows": other}
        )

    def place(half, shard, spot):
        start = pl.multiple_of((half * ndp + shard) * rows + spot[0], 16)
        return wbuf.at[pl.ds(start, spot[1])]

    def own_piece(part):
        first, size = pieces[part]
        return w_ref.at[pl.ds(pl.multiple_of(first, 16), size)]

    def z_copy(src, shard, part, side, step):
        target = right if side == 0 else left
        return remote(
            src,
            place(r, shard, pieces[part]),
            z_send.at[side, step, part],
            z_recv.at[side, step, part],
            {"dp": target},
        )

    def c_copy(shard, part, side, step):
        spot = place(r, shard, pieces[part])
        return remote(
            spot, spot, c_send.at[side, step, part], c_recv.at[side, step, part], {"rows": other}
        )

    def y_copy(shard, side, step):
        spot = place(r, shard, pieces[0])
        return remote(
            spot, spot, y_send.at[side, step], y_recv.at[side, step], {"tm": b_target}
        )

    def d_copy(shard, side, step):
        spot = place(r, shard, far_piece)
        return remote(spot, spot, d_send.at[side, step], d_recv.at[side, step], {"rows": other})

    def shard_of(step, side):
        return i - 1 - step if side == 0 else i + 1 + step

    def valid(step, side):
        shard = shard_of(step, side)
        return shard >= 0 if side == 0 else shard < ndp

    sends_on = (has_right, has_left)

    for part in range(parts):
        for side in (0, 1):
            @pl.when(sends_on[side])
            def _():
                z_copy(own_piece(part), i, part, side, 0).start()
    own_spot = wbuf.at[pl.ds(pl.multiple_of((r * ndp + i) * rows, 16), rows)]
    own_copy = pltpu.make_async_copy(w_ref, own_spot, own_local)
    own_copy.start()
    own_across = remote(w_ref, own_spot, own_send, own_recv, {"rows": other})
    own_across.start()
    loads[0].wait()
    for h in range(min(AHEAD, heads)):
        deinterleave(h)
        for s in (0, 1):
            a_copy(h, s).start()

    @pl.when(jnp.logical_not(has_b))
    def _():
        b_buf[...] = jnp.zeros_like(b_buf)

    for h in range(AHEAD, heads):
        deinterleave(h)

    if not relay:
        @pl.when(b_sends)
        def _():
            for h in range(heads):
                for s in (0, 1):
                    b_copy(h, s).start()

    def weight_event(step, part):
        for side in (0, 1):
            @pl.when(valid(step, side))
            def _():
                shard = shard_of(step, side)
                spot = place(r, shard, pieces[part])
                z_copy(spot, shard, part, side, step).wait_recv()

                @pl.when(sends_on[side])
                def _():
                    z_copy(spot, shard, part, side, step + 1).start()

                if shared and part == 0 and step == 0:
                    y_copy(shard, side, step).start()
                c_copy(shard, part, side, step).start()

    def relay_edge(step):
        for side in (0, 1):
            @pl.when(valid(step, side))
            def _():
                y_copy(shard_of(step, side), side, step).start()

    def far_event(step):
        for side in (0, 1):
            @pl.when(valid(step, side))
            def _():
                shard = shard_of(step, side)
                y_copy(shard, side, step).wait_recv()
                d_copy(shard, side, step).start()

    for load in loads[1:]:
        load.wait()

    def is_live(code):
        hit = off_ref[0] == code
        for k in range(1, off_ref.shape[0]):
            hit = jnp.logical_or(hit, off_ref[k] == code)
        return hit

    low = is_live(4)
    high = is_live(22)
    a_live = jnp.logical_or(jnp.logical_and(low, odd == 1), jnp.logical_and(high, odd == 0))
    b_live = jnp.logical_or(jnp.logical_and(low, odd == 0), jnp.logical_and(high, odd == 1))
    b_live = jnp.logical_and(b_live, has_b)
    dead = jnp.float32(-jnp.inf)
    a_bias = jnp.where(a_live, jnp.float32(0), dead)
    b_bias = jnp.where(b_live, jnp.float32(0), dead)
    factor = HD**-0.5 * math.log2(math.e)

    def score(q, keys):
        return lax.dot_general(
            q, keys, (((1,), (1,)), ((), ())), preferred_element_type=jnp.float32
        )

    def attend(g):
        h = head(g)
        q = q_ref[:, lanes(g)]
        held = (kv_ref, a_buf, b_buf)
        biases = (jnp.float32(0), a_bias, b_bias)
        scores = [score(q, buf[h, 0]) for buf in held]
        top = functools.reduce(
            jnp.maximum,
            [jnp.max(s, axis=1, keepdims=True) + bias for s, bias in zip(scores, biases)],
        )
        top = top * factor
        ones = jnp.ones((kv_in.shape[0], HD), jnp.bfloat16)
        acc = 0.0
        for s, bias, buf in zip(scores, biases, held):
            p = jnp.exp2(s * factor - (top - bias)).astype(jnp.bfloat16)
            values = jnp.concatenate([buf[h, 1], ones], axis=1)
            acc = acc + jnp.dot(p, values, preferred_element_type=jnp.float32)
        att_own[h] = (acc[:, :HD] / acc[:, HD:]).astype(jnp.bfloat16)
        across(g).start()

    width = out_ref.shape[1]
    tile = 512 if width % 512 == 0 else width
    mine = pl.ds(pl.multiple_of(r * band, 16), band)

    def project(p):
        first = p + descending * (heads // 2 - 1 - 2 * p)
        for g in (2 * p, 2 * p + 1):
            across(g).wait_recv()
        own = jnp.concatenate([att_own[2 * first + k, mine] for k in (0, 1)], axis=1)
        their = jnp.concatenate([att_other[2 * first + k] for k in (0, 1)], axis=1)
        for start in range(0, width, tile):
            columns = pl.ds(start, tile)
            value = 0.0
            for half, part in ((r, own), (other, their)):
                begin = pl.multiple_of(half * ndp * rows + first * 2 * HD, 2 * HD)
                value += jnp.dot(
                    part, wbuf[pl.ds(begin, 2 * HD), columns], preferred_element_type=jnp.float32
                )
            if p == 0:
                total_ref[:, columns] = value
            elif p < heads // 2 - 1:
                total_ref[:, columns] += value
            else:
                value = gate_ref[:, columns] * (total_ref[:, columns] + value)
                out_ref[:, columns] = value.astype(out_ref.dtype)

    def arrive(step):
        for side in (0, 1):
            @pl.when(valid(step, side))
            def _():
                shard = shard_of(step, side)
                for part in range(parts):
                    c_copy(shard, part, side, step).wait_recv()
                if shared:
                    d_copy(shard, side, step).wait_recv()

    staged = shared
    done = 0
    for h in range(heads + 1):
        if h < heads:
            for s in (0, 1):
                a_copy(h, s).wait_recv()
                if relay:
                    @pl.when(b_sends)
                    def _():
                        b_copy(h, s).start()
                if h + AHEAD < heads:
                    a_copy(h + AHEAD, s).start()
        if staged:
            for _ in range(PLAN.get(h, 0)):
                weight_event(done // parts, done % parts)
                done += 1
            if h == 2:
                far_event(0)
            if h == 5:
                relay_edge(1)
                relay_edge(2)
        if h > 0:
            g = h - 1

            @pl.when(has_b)
            def _():
                for s in (0, 1):
                    b_copy(g, s).wait_recv()

            attend(g)
            if staged and g == 3:
                own_copy.wait()
                own_across.wait_recv()
                arrive(0)
                project(0)

    if staged:
        far_event(1)
        weight_event(2, 2)
        arrive(1)
        project(1)
        far_event(2)
        arrive(2)
        project(2)
    else:
        def advance(step, carry):
            for part in range(parts):
                weight_event(step, part)
            return carry

        lax.fori_loop(0, steps, advance, 0)
        own_copy.wait()
        own_across.wait_recv()
        lax.fori_loop(0, steps, lambda step, carry: (arrive(step), carry)[1], 0)
        for p in range(heads // 2):
            project(p)

    for h in range(heads):
        across(h).wait_send()
        for s in (0, 1):
            a_copy(h, s).wait_send()

    @pl.when(b_sends)
    def _():
        for h in range(heads):
            for s in (0, 1):
                b_copy(h, s).wait_send()

    own_across.wait_send()

    for part in range(parts):
        for side in (0, 1):
            @pl.when(sends_on[side])
            def _():
                z_copy(own_piece(part), i, part, side, 0).wait_send()

    def sent(step, carry):
        for side in (0, 1):
            @pl.when(valid(step, side))
            def _():
                shard = shard_of(step, side)
                for part in range(parts):
                    c_copy(shard, part, side, step).wait_send()

                    @pl.when(sends_on[side])
                    def _():
                        spot = place(r, shard, pieces[part])
                        z_copy(spot, shard, part, side, step + 1).wait_send()

                if shared:
                    y_copy(shard, side, step).wait_send()
                    d_copy(shard, side, step).wait_send()
        return carry

    lax.fori_loop(0, steps, sent, 0)


def local(queries, keys_values, window_offsets, out_weight, gate):
    tl, width = queries.shape[4], queries.shape[5]
    heads = width // HD
    ndp, ntm, bands = lax.axis_size("dp"), lax.axis_size("tm"), lax.axis_size("rows")
    assert queries.shape[2] == queries.shape[3] == 1 and bands == 2 and ntm % 2 == 0 and heads % 2 == 0
    band = tl // bands
    rows, dout = out_weight.shape
    kv = keys_values.reshape(tl, 2, width)
    bf16 = jnp.bfloat16
    vmem = pl.BlockSpec(memory_space=pltpu.VMEM)
    hbm = pl.BlockSpec(memory_space=pltpu.HBM)
    dma = pltpu.SemaphoreType.DMA
    mixed = pl.pallas_call(
        functools.partial(kernel, ndp, ntm, heads),
        out_shape=jax.ShapeDtypeStruct((band, dout), bf16),
        in_specs=[hbm] * 5,
        out_specs=vmem,
        scratch_shapes=[
            pltpu.SMEM((window_offsets.size,), jnp.int32),
            pltpu.VMEM((tl, width), bf16),
            pltpu.VMEM((tl, 2, width), bf16),
            pltpu.VMEM((1, dout), jnp.float32),
            pltpu.VMEM((heads, 2, tl, HD), bf16),
            pltpu.VMEM((heads, 2, tl, HD), bf16),
            pltpu.VMEM((heads, 2, tl, HD), bf16),
            pltpu.VMEM((2 * ndp * rows, dout), bf16),
            pltpu.VMEM((heads, tl, HD), bf16),
            pltpu.VMEM((heads, band, HD), bf16),
            pltpu.VMEM((band, dout), jnp.float32),
            dma((heads, 2)),
            dma((heads, 2)),
            dma((heads, 2)),
            dma((heads, 2)),
            dma((2, ndp, 3)),
            dma((2, ndp, 3)),
            dma((2, ndp, 3)),
            dma((2, ndp, 3)),
            dma((2, ndp)),
            dma((2, ndp)),
            dma((2, ndp)),
            dma((2, ndp)),
            dma,
            dma,
            dma,
            dma((heads,)),
            dma((heads,)),
            dma((4,)),
        ],
        compiler_params=pltpu.CompilerParams(
            collective_id=0, has_side_effects=True, vmem_limit_bytes=64 * 1024 * 1024
        ),
        cost_estimate=pl.CostEstimate(
            flops=4 * 3 * tl * tl * width + 4 * band * width * dout,
            bytes_accessed=2 * (3 * tl * width + rows * dout + band * dout),
            transcendentals=3 * tl * tl * heads,
        ),
    )(window_offsets.reshape(-1), queries.reshape(tl, width), kv, out_weight, gate)
    return mixed.reshape(1, 1, 1, 1, band, dout)


def solution(mesh):
    placed = (
        P("dp", "tm", None, None, None, "rows"),
        P("dp", "tm", None, None, None, None, "rows"),
        P("dp", "tm", None, None, None),
        P(("rows", "dp"), None),
        P("dp", None),
    )
    return jax.shard_map(
        local,
        mesh=mesh,
        in_specs=placed,
        out_specs=P("dp", "tm", None, None, "rows", None),
        check_vma=False,
    )
```
